256 devices in a mesh: fsdp: 16 (over z, core), rep: 16 (over y, x).
Axes of the slice: x: 4, y: 4, z: 8, core: 2. Of those that a mesh axis runs over, the one named last changes fastest.
Arguments:
- inputs: bfloat16 [32768, 256], P(('fsdp', 'rep')), may hold values from -6 to 6
- cotangent: bfloat16 [32768, 28672], P(('fsdp', 'rep')), may hold values from -0.5 to 0.5
- momentum: float32 [16, 28672, 256], P('rep', 'fsdp'), may hold values from -12 to 12
- coef_index: int32 [16, 448, 4, 32], P('rep', 'fsdp'), may hold values from 0 to 4095, as said below
- counts: int32 [16, 448, 4], P('rep', 'fsdp'), may hold values from 8 to 32, as said below
Outputs:
- new_momentum: float32 [16, 28672, 256], P('rep', 'fsdp')
- update: float32 [28672, 256], P('fsdp')
The draws below stay inside these ranges and needn't reach their ends.
Inputs may be any that keep to these rules, and one draw needn't show every extreme that they name: `coef_index`: the 32 frequencies listed for one group of one replica are all different. `counts`: every replica has a group with all 32 slots valid.
All inputs are finite; a program needn't handle non-finite values.
Results may differ from the reference program's by a relative error of at most 0.0003.
Values may be sent and summed in bfloat16 or wider, within the bound.
No kernel may reach another device: no remote copies, remote signals or barrier semaphores. Data moves between devices by JAX's collectives and lax.ppermute only.
A program may use at most 128 MiB of HBM per device.

```python
import math
import jax
import jax.numpy as jnp
from jax import lax

FF = 28672
COLS = 256
TOK_DEV = 128
GROUP = 64
TOPK = 32
TOKENS = 32768
N_FSDP = 16
N_REP = 16


def draw_coef_index(key, part):
    key = jax.random.fold_in(key, 11)
    shape = (N_REP, FF // GROUP, COLS // GROUP, GROUP * GROUP)
    scores = jax.random.randint(key, shape, 0, 2 ** 18) * (GROUP * GROUP) + lax.broadcasted_iota(jnp.int32, shape, 3)
    return lax.top_k(scores, TOPK)[1].astype(jnp.int32)


def draw_counts(key, part):
    key = jax.random.fold_in(key, 23)
    key_base, key_spot = jax.random.split(key)
    shape = (N_REP, FF // GROUP, COLS // GROUP)
    drawn = jax.random.randint(key_base, shape, TOPK // 4, TOPK + 1)
    chosen = jax.random.randint(key_spot, (N_REP, 1, 1), 0, FF // GROUP * (COLS // GROUP))
    flat_ids = lax.broadcasted_iota(jnp.int32, shape, 1) * (COLS // GROUP) + lax.broadcasted_iota(jnp.int32, shape, 2)
    return jnp.where(flat_ids == chosen, TOPK, drawn).astype(jnp.int32)


def strengthened(result, key, source, target, parts, factor):
    owner, partner = [(jnp.arange(result.shape[dim]) // (result.shape[dim] // parts)).reshape([-1 if axis == dim else 1 for axis in range(result.ndim)]) for dim in (source, target)]
    chosen = jax.random.permutation(key, parts)[partner]
    strong = (owner == chosen) | (owner == (partner + parts // 2) % parts)
    return jnp.where(strong, factor * result, result)


def level_of(rng, extent, cuts, smallest, high):
    gain = 1.0
    for axis_at, blocks in cuts:
        heights = jax.random.uniform(jax.random.fold_in(jax.random.fold_in(rng, 6), axis_at), (blocks,), jnp.float32, smallest / len(cuts), high / len(cuts))
        gain = gain * jnp.repeat(jnp.exp(heights), extent[axis_at] // blocks).reshape((-1,) + (1,) * (len(extent) - 1 - axis_at))
    return gain


def gaussian(key, extent, deviation, most, cuts=(), kind=jnp.bfloat16):
    level = level_of(key, extent, cuts, -0.22, 0.18) if cuts else 1.0
    values = jax.random.normal(key, extent, jnp.float32) * deviation * level
    return jnp.minimum(jnp.maximum(values, -most), most).astype(kind)


def noise_with(stream_key, dims, scale, reach, shards, heavy, kind=jnp.bfloat16):
    array = scale * jax.random.normal(stream_key, dims, jnp.float32)
    if shards:
        array = array * level_of(stream_key, dims, shards, -0.22, 0.18)
    return jnp.clip(strengthened(array, jax.random.fold_in(stream_key, 3), *heavy), -reach, reach).astype(kind)


def setup_inputs(seed: int = 0) -> dict:
    keys = jax.random.split(jax.random.key(seed), 6)
    return {
        "inputs": gaussian(keys[0], (TOKENS, COLS), 1.0, 6.0, ((0, 256),)),
        "cotangent": noise_with(keys[1], (TOKENS, FF), (TOK_DEV * N_FSDP) ** -0.5, 0.5, ((0, 256),), (0, 1, 256, 6.0)),
        "momentum": gaussian(keys[2], (N_REP, FF, COLS), 2.0, 12.0, ((0, 16), (1, 16)), jnp.float32),
        "coef_index": draw_coef_index(jax.random.fold_in(keys[5], 71), 0),
        "counts": draw_counts(jax.random.fold_in(keys[5], 71), 0),
    }


decay_rate = 0.9

def cosine_table(group_size):
    freq = jnp.arange(group_size, dtype=jnp.float32)[:, None]
    place_ids = jnp.arange(group_size, dtype=jnp.float32)[None, :]
    cosines = jnp.cos(math.pi * (2.0 * place_ids + 1.0) * freq / (2.0 * group_size)) * math.sqrt(2.0 / group_size)
    scaling = jnp.where(jnp.arange(group_size) == 0, math.sqrt(0.5), 1.0).astype(cosines.dtype)
    return cosines * scaling[:, None]

def forward_groups(matrix_tile, cosines):
    group_size = cosines.shape[0]
    height, width = matrix_tile.shape
    grouped = matrix_tile.reshape(height // group_size, group_size, width // group_size, group_size)
    spectrum = jnp.einsum('un,anbm,wm->abuw', cosines, grouped, cosines, precision=lax.Precision.HIGHEST)
    return spectrum.reshape(height // group_size, width // group_size, group_size * group_size)

def inverse_groups(spectrum, cosines):
    group_size = cosines.shape[0]
    across, down_count, _ = spectrum.shape
    square = spectrum.reshape(across, down_count, group_size, group_size)
    grouped = jnp.einsum('un,abuw,wm->anbm', cosines, square, cosines, precision=lax.Precision.HIGHEST)
    return grouped.reshape(across * group_size, down_count * group_size)

def place_values(kept_values, positions, total_slots):
    across, down_count, slot_count = positions.shape
    group_ids = jnp.arange(across * down_count, dtype=jnp.int32)[:, None]
    dense_sum = jnp.zeros((across * down_count, total_slots), jnp.float32)
    dense_sum = dense_sum.at[group_ids, positions.reshape(across * down_count, slot_count)].add(kept_values.reshape(across * down_count, slot_count))
    return dense_sum.reshape(across, down_count, total_slots)

def reference(inputs, cotangent, momentum, coef_index, counts):
    cosines = cosine_table(GROUP)
    by_replica_in = inputs.reshape(N_FSDP, N_REP, TOK_DEV, COLS).transpose(1, 0, 2, 3).reshape(N_REP, N_FSDP * TOK_DEV, COLS)
    by_replica_cot = cotangent.reshape(N_FSDP, N_REP, TOK_DEV, FF).transpose(1, 0, 2, 3).reshape(N_REP, N_FSDP * TOK_DEV, FF)

    def one_replica(packed):
        rep_inputs, rep_cot, rep_momentum, rep_index, rep_counts = packed
        gradient = jnp.dot(rep_cot.T, rep_inputs, preferred_element_type=jnp.float32)
        updated = decay_rate * rep_momentum + gradient
        spectrum = forward_groups(updated, cosines)
        picked = jnp.take_along_axis(spectrum, rep_index, axis=2)
        slot_ids = jnp.arange(TOPK, dtype=jnp.int32)[None, None, :]
        kept_values = jnp.where(slot_ids < rep_counts[:, :, None], picked, 0.0)
        decoded = inverse_groups(place_values(kept_values, rep_index, GROUP * GROUP), cosines)
        return (updated - decoded, decoded)
    new_momentum, decoded = lax.map(one_replica, (by_replica_in, by_replica_cot, momentum, coef_index, counts))
    return (new_momentum, lax.optimization_barrier(jnp.sum(decoded, axis=0)))
```

```python
import functools
import math

import jax
import jax.numpy as jnp
import numpy as np
from jax import lax
from jax.experimental import pallas as pl
from jax.experimental.pallas import tpu as pltpu
from jax.sharding import PartitionSpec as P

GROUP = 64
DECAY = 0.9
CHIPS = 8
TOK = 128
COLS = 256
ROWS = 1792
HALF = 896
TILES = HALF // 128
MSG = TILES * COLS + 16
PAIRS = ROWS // 128
N_REP = 16
STEP = 64.0
TOP = 32760.0
HIGH = lax.Precision.HIGHEST
F32 = jnp.float32
BF16 = jnp.bfloat16
VMEM_LIMIT = 40 * 1024 * 1024


def cosine_table():
    freq = np.arange(GROUP)[:, None]
    place = np.arange(GROUP)[None, :]
    table = np.cos(math.pi * (2.0 * place + 1.0) * freq / (2.0 * GROUP)) * math.sqrt(2.0 / GROUP)
    table[0] *= math.sqrt(0.5)
    return table.astype(np.float32)


def call(kernel, out_shape, flops, nbytes, name, **kw):
    return pl.pallas_call(
        kernel,
        out_shape=out_shape,
        name=name,
        compiler_params=pltpu.CompilerParams(vmem_limit_bytes=VMEM_LIMIT),
        cost_estimate=pl.CostEstimate(flops=flops, bytes_accessed=nbytes, transcendentals=0),
        **kw,
    )


def read_scales(msg):
    codes = msg[TILES * COLS : MSG, :].astype(F32)
    return jnp.exp2(codes * (1.0 / STEP)) * (1.0 / TOP)


def read_tile(msg, scales, j):
    return msg[j * COLS : (j + 1) * COLS, :].astype(F32) * scales[j : j + 1, :]


def partial_tile(in_own, in_sib, own, sib, j):
    cols = slice(j * 128, (j + 1) * 128)
    return jnp.dot(in_own, own[:, cols], preferred_element_type=F32) + jnp.dot(
        in_sib, sib[:, cols], preferred_element_type=F32
    )


def write_message(out, tiles):
    codes = []
    for j, tile in enumerate(tiles):
        top = jnp.maximum(jnp.max(jnp.abs(tile), axis=0, keepdims=True), 1e-30)
        code = jnp.ceil(jnp.log2(top) * STEP)
        inv = jnp.exp2(code * (-1.0 / STEP)) * TOP
        out[j * COLS : (j + 1) * COLS, :] = jnp.round(tile * inv).astype(jnp.int32).astype(jnp.int16)
        codes.append(code)
    codes.append(jnp.zeros((16 - len(codes), 128), F32))
    out[TILES * COLS : MSG, :] = jnp.concatenate(codes, axis=0).astype(jnp.int32).astype(jnp.int16)


def hop_kernel(has_recv, in_own, in_sib, own_f, sib_f, own_b, sib_b, *refs):
    a, b = in_own[...], in_sib[...]
    recvs = refs[:2] if has_recv else (None, None)
    outs = refs[-2:]
    for own, sib, recv, out in ((own_f, sib_f, recvs[0], outs[0]), (own_b, sib_b, recvs[1], outs[1])):
        scales = read_scales(recv) if has_recv else None
        tiles = []
        for j in range(TILES):
            tile = partial_tile(a, b, own, sib, j)
            if has_recv:
                tile = tile + read_tile(recv, scales, j)
            tiles.append(tile)
        write_message(out, tiles)


def hop(inputs, blocks, recvs, name):
    out = jax.ShapeDtypeStruct((MSG, 128), jnp.int16)
    return call(
        functools.partial(hop_kernel, bool(recvs)),
        (out, out),
        4 * 2 * TOK * COLS * HALF,
        6 * 2 * TOK * HALF * 2,
        name,
    )(*inputs, *blocks, *recvs)


def basis_kernel(u_ref, cos_t, out):
    row = lax.broadcasted_iota(jnp.int32, (128, 256), 0)
    lane = lax.broadcasted_iota(jnp.int32, (128, 256), 1)
    shift = jnp.where(lane >= 128, GROUP, 0)
    for p in range(PAIRS):
        onehot = jnp.where(row == u_ref[p : p + 1, :] + shift, 1.0, 0.0).astype(F32)
        out[p * 128 : (p + 1) * 128, :] = jnp.dot(
            cos_t[...], onehot, precision=HIGH, preferred_element_type=F32
        )


def kept_kernel(in_own, in_sib, own, sib, recv_f, recv_b, mom_t, basis, w_ref, valid, cos4, updated, kept):
    a, b = in_own[...], in_sib[...]
    scales_f, scales_b = read_scales(recv_f), read_scales(recv_b)
    row = lax.broadcasted_iota(jnp.int32, (COLS, 256), 0)
    for j in range(TILES):
        cols = slice(j * 128, (j + 1) * 128)
        tile = partial_tile(a, b, own, sib, j) + mom_t[:, cols]
        tile = tile + read_tile(recv_f, scales_f, j) + read_tile(recv_b, scales_b, j)
        updated[:, cols] = tile
        half = jnp.dot(cos4[...], tile, precision=HIGH, preferred_element_type=F32)
        full = jnp.dot(
            half, basis[j * 128 : (j + 1) * 128, :], precision=HIGH, preferred_element_type=F32
        )
        picked = jnp.sum(jnp.where(row == w_ref[j : j + 1, :], full, 0.0), axis=0, keepdims=True)
        kept[j : j + 1, :] = jnp.where(valid[j : j + 1, :] > 0.0, picked, 0.0)


def own_kernel(updated, kept, w_ref, basis, cos4_t, out):
    row = lax.broadcasted_iota(jnp.int32, (COLS, 256), 0)
    p = pl.program_id(0)
    placed = jnp.where(row == w_ref[pl.ds(p, 1), :], kept[pl.ds(p, 1), :], 0.0)
    spread = lax.dot_general(
        placed, basis[...], (((1,), (1,)), ((), ())), precision=HIGH, preferred_element_type=F32
    )
    decoded = jnp.dot(cos4_t[...], spread, precision=HIGH, preferred_element_type=F32)
    out[...] = (updated[...] - decoded).T


def update_kernel(kept, idx, cos4, cos4_t, out):
    g = pl.program_id(0)
    row_u = lax.broadcasted_iota(jnp.int32, (128, 256), 0) & (GROUP - 1)
    upper = lax.broadcasted_iota(jnp.int32, (128, 256), 0) < GROUP
    row_w = lax.broadcasted_iota(jnp.int32, (COLS, 256), 0)
    lane = lax.broadcasted_iota(jnp.int32, (1, 256), 1)
    offset = ((lane & 127) >> 5) * GROUP
    groups = []
    for i in range(4):
        at = pl.ds(g * 4 + i, 1)
        total = jnp.zeros((128, 256), F32)
        for r in range(0, N_REP, 2):
            k = jnp.concatenate([kept[r, at, :], kept[r + 1, at, :]], axis=1)
            n = jnp.concatenate([idx[r, at, :], idx[r + 1, at, :]], axis=1)
            k_high = k.astype(BF16).astype(F32)
            k_low = k - k_high
            left = jnp.where(row_u == (n >> 6), jnp.where(upper, k_high, k_low), 0.0).astype(BF16)
            right = jnp.where(row_w == (n & 63) + offset, 1.0, 0.0).astype(BF16)
            total = total + lax.dot_general(
                left, right, (((1,), (1,)), ((), ())), preferred_element_type=F32
            )
        groups.append(total[:GROUP] + total[GROUP:])
    dense = jnp.concatenate(groups, axis=0)
    half = jnp.dot(cos4_t[...], dense, precision=HIGH, preferred_element_type=F32)
    out[...] = jnp.dot(half, cos4[...], precision=HIGH, preferred_element_type=F32)


def chip_perm(dz, flip=False):
    return [
        (2 * z + c, 2 * ((z + dz) % CHIPS) + (1 - c if flip else c))
        for z in range(CHIPS)
        for c in range(2)
    ]


def rep_perm(dx, dy):
    return [(i, ((i // 4 + dy) % 4) * 4 + (i % 4 + dx) % 4) for i in range(N_REP)]


def gather_rep(kept):
    row = jnp.stack([kept] + [lax.ppermute(kept, "rep", rep_perm(dx, 0)) for dx in (1, 2, 3)])
    return jnp.concatenate([row] + [lax.ppermute(row, "rep", rep_perm(0, dy)) for dy in (1, 2, 3)])


def on_device(inputs, cotangent, momentum, coef_index, counts):
    cosines = cosine_table()
    cos4 = jnp.asarray(np.kron(np.eye(4, dtype=np.float32), cosines))
    cos4_t = jnp.asarray(np.kron(np.eye(4, dtype=np.float32), cosines.T))
    cos2_t = jnp.asarray(np.kron(np.eye(2, dtype=np.float32), cosines.T))

    place = lax.axis_index("fsdp")
    z, core = place // 2, place % 2

    def block(k, of_core):
        start = (2 * ((z + k) % CHIPS) + of_core) * ROWS
        return lax.dynamic_slice(cotangent, (0, start), (TOK, ROWS))

    order = (4, 3, 5, 2, 6, 1, 7, 0)
    swap = lambda x: lax.ppermute(x, "fsdp", chip_perm(0, True))
    first = swap(jnp.concatenate([block(4, 1 - core), inputs], axis=1))
    second = swap(jnp.concatenate([block(k, 1 - core) for k in order[1:3]], axis=1))
    third = swap(jnp.concatenate([block(k, 1 - core) for k in order[3:]], axis=1))
    in_t = (inputs.T, first[:, ROWS:].T)
    theirs = {4: first[:, :ROWS]}
    for n, k in enumerate(order[1:3]):
        theirs[k] = second[:, n * ROWS : (n + 1) * ROWS]
    for n, k in enumerate(order[3:]):
        theirs[k] = third[:, n * ROWS : (n + 1) * ROWS]
    halves = lambda k, h: (
        block(k, core)[:, h * HALF : (h + 1) * HALF],
        theirs[k][:, h * HALF : (h + 1) * HALF],
    )

    index = coef_index[0].reshape(ROWS // GROUP, 128)
    index_all = gather_rep(index)
    lanes = jnp.arange(128, dtype=jnp.int32)
    freq_u = (index >> 6).reshape(PAIRS, 256)
    freq_w = ((index & 63) + (lanes // 32 * GROUP)[None, :]).reshape(PAIRS, 256)
    valid = (lanes % 32)[None, :] < jnp.repeat(counts[0], 32, axis=1)
    valid = valid.astype(F32).reshape(PAIRS, 256)
    mom_t = (DECAY * momentum[0]).T
    basis = call(
        basis_kernel,
        jax.ShapeDtypeStruct((ROWS, 256), F32),
        6 * 2 * PAIRS * 128 * 128 * 256,
        ROWS * 256 * 4,
        "basis",
    )(freq_u, cos2_t)

    sent = []
    for slot in range(7):
        h = slot % 2
        k = 4 - (slot + 1) // 2
        blocks = halves(k, h) + halves(CHIPS - k, 1 - h)
        recvs = sent[slot - 2] if slot >= 2 else ()
        forth, back = hop(in_t, blocks, recvs, "hop%d" % slot)
        sent.append(
            (
                lax.ppermute(forth, "fsdp", chip_perm(1)),
                lax.ppermute(back, "fsdp", chip_perm(-1)),
            )
        )
    arrived = ((sent[6][0], sent[5][1]), (sent[5][0], sent[6][1]))

    updated, kept = [], []
    for h in range(2):
        rows = slice(h * TILES, (h + 1) * TILES)
        upd, kep = call(
            kept_kernel,
            (
                jax.ShapeDtypeStruct((COLS, HALF), F32),
                jax.ShapeDtypeStruct((TILES, 256), F32),
            ),
            6 * 2 * TILES * (256 * 256 * 128 + 256 * 128 * 256),
            5 * HALF * 256 * 4,
            "kept%d" % h,
        )(
            *in_t,
            *halves(0, h),
            *arrived[h],
            mom_t[:, h * HALF : (h + 1) * HALF],
            basis[h * HALF : (h + 1) * HALF],
            freq_w[rows],
            valid[rows],
            cos4,
        )
        updated.append(upd)
        kept.append(kep)
    updated = jnp.concatenate(updated, axis=1)
    kept = jnp.concatenate(kept, axis=0)

    kept_all = gather_rep(kept.reshape(ROWS // GROUP, 128))

    whole = lambda shape: pl.BlockSpec(shape, lambda g: (0,) * len(shape))
    new_momentum = call(
        own_kernel,
        jax.ShapeDtypeStruct((ROWS, COLS), F32),
        6 * 2 * PAIRS * (256 * 256 * 128 * 2),
        3 * ROWS * 256 * 4,
        "own",
        grid=(PAIRS,),
        in_specs=[
            pl.BlockSpec((COLS, 128), lambda g: (0, g)),
            whole((PAIRS, 256)),
            whole((PAIRS, 256)),
            pl.BlockSpec((128, 256), lambda g: (g, 0)),
            whole((256, 256)),
        ],
        out_specs=pl.BlockSpec((128, COLS), lambda g: (g, 0)),
    )(updated, kept, freq_w, basis, cos4_t)

    update = call(
        update_kernel,
        jax.ShapeDtypeStruct((ROWS, COLS), F32),
        2 * 28 * 128 * 2048 * 256,
        ROWS * 256 * 4,
        "update",
        grid=(7,),
        in_specs=[
            whole((N_REP, 28, 128)),
            whole((N_REP, 28, 128)),
            whole((256, 256)),
            whole((256, 256)),
        ],
        out_specs=pl.BlockSpec((256, COLS), lambda g: (g, 0)),
    )(kept_all, index_all, cos4, cos4_t)
    return new_momentum[None], update


def solution(mesh):
    return jax.shard_map(
        on_device,
        mesh=mesh,
        in_specs=(
            P(("fsdp", "rep"), None),
            P(("fsdp", "rep"), None),
            P("rep", "fsdp", None),
            P("rep", "fsdp", None, None),
            P("rep", "fsdp", None),
        ),
        out_specs=(P("rep", "fsdp", None), P("fsdp", None)),
        check_vma=False,
    )
```

```python
import functools
import math

import jax
import jax.numpy as jnp
import numpy as np
from jax import lax
from jax.experimental import pallas as pl
from jax.experimental.pallas import tpu as pltpu
from jax.sharding import PartitionSpec as P

GROUP = 64
DECAY = 0.9
CHIPS = 8
TOK = 128
COLS = 256
ROWS = 1792
HALF = 896
TILES = ROWS // 128
GROUPS = ROWS // GROUP
HALF_GROUPS = GROUPS // 2
GROUPS = ROWS // GROUP
HALF_GROUPS = GROUPS // 2
MSG = TILES * COLS + 16
N_REP = 16
STEP = 64.0
TOP = 32760.0
HIGH = lax.Precision.HIGHEST
F32 = jnp.float32
BF16 = jnp.bfloat16
SLOTS = (
    (4, False),
    (3, True),
    (3, False),
    (2, True),
    (2, False),
    (1, True),
    (1, False),
    (0, False),
)
VMEM_LIMIT = 24 * 1024 * 1024


def cosine_table():
    freq = np.arange(GROUP)[:, None]
    place = np.arange(GROUP)[None, :]
    table = np.cos(math.pi * (2.0 * place + 1.0) * freq / (2.0 * GROUP)) * math.sqrt(2.0 / GROUP)
    table[0] *= math.sqrt(0.5)
    return table.astype(np.float32)


def call(kernel, out_shape, name, grid, in_specs, out_specs, scalars=0, scratch=(), flops=235_000_000, nbytes=1_400_000):
    return pl.pallas_call(
        kernel,
        out_shape=out_shape,
        name=name,
        grid_spec=pltpu.PrefetchScalarGridSpec(
            num_scalar_prefetch=scalars,
            grid=grid,
            in_specs=in_specs,
            out_specs=out_specs,
            scratch_shapes=scratch,
        ),
        compiler_params=pltpu.CompilerParams(vmem_limit_bytes=VMEM_LIMIT),
        cost_estimate=pl.CostEstimate(flops=flops, bytes_accessed=nbytes, transcendentals=0),
    )


def whole(*shape):
    return pl.BlockSpec(shape, lambda *_: (0,) * len(shape))


AFTER = pl.BlockSpec(memory_space=pl.ANY)


def split(x):
    high = x.astype(BF16)
    return high, (x - high.astype(F32)).astype(BF16)


def read_scales(msg):
    codes = msg[TILES * COLS : MSG, :].astype(F32)
    return jnp.exp2(codes * (1.0 / STEP)) * (1.0 / TOP)


def read_tile(msg, scales, j):
    return msg[j * COLS : (j + 1) * COLS, :].astype(F32) * scales[j : j + 1, :]


def partial_tile(in_t, own, sib, j):
    cols = slice(j * 128, (j + 1) * 128)
    tokens = jnp.concatenate([own[:, cols], sib[:, cols]], axis=0)
    return jnp.dot(in_t, tokens, preferred_element_type=F32)


def write_message(out, tiles):
    codes = []
    for j, tile in enumerate(tiles):
        top = jnp.maximum(jnp.max(jnp.abs(tile), axis=0, keepdims=True), 1e-30)
        code = jnp.ceil(jnp.log2(top) * STEP)
        inv = jnp.exp2(code * (-1.0 / STEP)) * TOP
        out[j * COLS : (j + 1) * COLS, :] = jnp.round(tile * inv).astype(jnp.int32).astype(jnp.int16)
        codes.append(code)
    codes.append(jnp.zeros((16 - len(codes), 128), F32))
    out[TILES * COLS : MSG, :] = jnp.concatenate(codes, axis=0).astype(jnp.int32).astype(jnp.int16)


def copy_kernel(slots, cot, extra, send, own, sems):
    place = lax.axis_index("fsdp")
    chip, core = place // 2, place % 2
    copies = []
    for whose, out in ((1 - core, send), (core, own)):
        for n, (k, flip) in enumerate(slots if out is not None else ()):
            to = (chip + k * (1 - 2 * whose) + CHIPS) % CHIPS
            start = pl.multiple_of((2 * to + (1 - whose if flip else whose)) * ROWS, 128)
            for row in range(0, TOK, 32):
                rows = slice(row, row + 32)
                copies.append(
                    (
                        cot.at[rows, pl.ds(start, ROWS)],
                        out.at[rows, n * ROWS : (n + 1) * ROWS],
                        sems.at[len(copies)],
                    )
                )
    copies = [pltpu.make_async_copy(*c) for c in copies]
    for c in copies:
        c.start()
    if extra is not None:
        send[:, len(slots) * ROWS :] = extra[...]
    for c in copies:
        c.wait()


def first_copy_kernel(cot, extra, send, own, sems):
    copy_kernel(SLOTS[:1], cot, extra, send, own, sems)


def later_copy_kernel(slots, cot, after, send, own, sems):
    copy_kernel(slots, cot, None, send, own, sems)


def first_hop_kernel(in_own, in_sib, own, sib, after, in_t, out):
    in_t[:, :TOK] = in_own[...].astype(F32).T.astype(BF16)
    in_t[:, TOK:] = in_sib[...].astype(F32).T.astype(BF16)
    both = in_t[...]
    write_message(out, [partial_tile(both, own, sib, j) for j in range(TILES)])


def hop_kernel(n_after, *refs):
    in_t, own, sib, *recv, out = refs[n_after:]
    both = in_t[...]
    tiles = [partial_tile(both, own, sib, j) for j in range(TILES)]
    if recv:
        scales = read_scales(recv[0])
        tiles = [tile + read_tile(recv[0], scales, j) for j, tile in enumerate(tiles)]
    write_message(out, tiles)


def tables_kernel(listed, counts, cos_t, after, basis, cw, valid, places):
    row = lax.broadcasted_iota(jnp.int32, (GROUP, 512), 0)
    lane = lax.broadcasted_iota(jnp.int32, (GROUP, 256), 1)
    index = jnp.concatenate([listed[:, j, :] for j in range(4)], axis=1)
    places[...] = index.astype(F32)
    for p in range(TILES):
        n = jnp.concatenate([index[2 * p : 2 * p + 1, :], index[2 * p + 1 : 2 * p + 2, :]], axis=1)
        onehot = jnp.where(row == jnp.concatenate([n >> 6, n & 63], axis=1), 1.0, 0.0).astype(F32)
        both = jnp.dot(cos_t[...], onehot, precision=HIGH, preferred_element_type=F32)
        cw[p * GROUP : (p + 1) * GROUP, :] = both[:, 256:]
        cu = both[:, :256]
        diagonal = jnp.concatenate(
            [jnp.where(lane < 128, cu, 0.0), jnp.where(lane >= 128, cu, 0.0)], axis=0
        )
        high, low = split(diagonal)
        basis[p * 256 : p * 256 + 128, :] = high
        basis[p * 256 + 128 : (p + 1) * 256, :] = low
    slot = lax.broadcasted_iota(jnp.int32, (GROUPS, 128), 1)
    limit = jnp.zeros((GROUPS, 128), jnp.int32)
    for j in range(4):
        limit = jnp.where((slot >> 5) == j, counts[:, j : j + 1], limit)
    valid[...] = jnp.where((slot & 31) < limit, 1.0, 0.0).astype(F32)


def momentum_kernel(momentum, after, out):
    out[...] = (DECAY * momentum[...]).T


def by_column_group(rows):
    block = lax.broadcasted_iota(jnp.int32, rows[0].shape, 1) >> 5
    out = []
    for j in range(4):
        total = rows[j]
        for b in range(4):
            if b != j:
                total = jnp.where(block == b, pltpu.roll(rows[b], (32 * (b - j)) % 128, 1), total)
        out.append(total)
    return out


def base_kernel(in_t, own, sib, msg, mom_t, out):
    both = in_t[...]
    scales = read_scales(msg)
    for j in range(TILES):
        cols = slice(j * 128, (j + 1) * 128)
        out[:, cols] = partial_tile(both, own, sib, j) + mom_t[:, cols] + read_tile(msg, scales, j)


def kept_kernel(msg, base, basis, cw, valid, places, updated, kept):
    kept[GROUPS:, :] = places[...]
    column = (lax.broadcasted_iota(jnp.int32, (GROUP, 256), 1) & 127) >> 5
    scales = read_scales(msg)
    for p in range(TILES):
        cols = slice(p * 128, (p + 1) * 128)
        tile = base[:, cols] + read_tile(msg, scales, p)
        updated[:, cols] = tile
        high, low = split(tile)
        b_high = basis[p * 256 : p * 256 + 128, :]
        b_low = basis[p * 256 + 128 : (p + 1) * 256, :]
        seen = jnp.dot(
            jnp.concatenate([high, low, high], axis=1),
            jnp.concatenate([b_high, b_high, b_low], axis=0),
            preferred_element_type=F32,
        )
        mine = seen[:GROUP]
        for c in range(1, 4):
            mine = jnp.where(column == c, seen[c * GROUP : (c + 1) * GROUP], mine)
        picked = jnp.sum(mine * cw[p * GROUP : (p + 1) * GROUP, :], axis=0, keepdims=True)
        for i in range(2):
            at = slice(2 * p + i, 2 * p + i + 1)
            half = picked[:, i * 128 : (i + 1) * 128]
            kept[at, :] = jnp.where(valid[at, :] > 0.0, half, 0.0)


def own_kernel(updated, kept, basis, cw, out):
    g = pl.program_id(0)
    column = (lax.broadcasted_iota(jnp.int32, (GROUP, 256), 1) & 127) >> 5
    for p in range(TILES // 2):
        k = jnp.concatenate(
            [kept[pl.ds(2 * (g * (TILES // 2) + p) + i, 1), :] for i in range(2)], axis=1
        )
        weighted = cw[p * GROUP : (p + 1) * GROUP, :] * k
        spread = jnp.concatenate([jnp.where(column == c, weighted, 0.0) for c in range(4)], axis=0)
        high, low = split(spread)
        b_high = basis[p * 256 : p * 256 + 128, :]
        b_low = basis[p * 256 + 128 : (p + 1) * 256, :]
        decoded = lax.dot_general(
            jnp.concatenate([high, low, high], axis=1),
            jnp.concatenate([b_high, b_high, b_low], axis=1),
            (((1,), (1,)), ((), ())),
            preferred_element_type=F32,
        )
        cols = slice(p * 128, (p + 1) * 128)
        out[cols, :] = (updated[:, cols] - decoded).T


def update_kernel(k0, k1, k2, k3, cos_t3, cos4_3, out, kept, index):
    g = pl.program_id(0)

    @pl.when(g == 0)
    def _():
        for y, ref in enumerate((k0, k1, k2, k3)):
            for rows, arranged in ((slice(0, GROUPS), kept), (slice(GROUPS, 2 * GROUPS), index)):
                groups = by_column_group([ref[x, rows, :] for x in range(4)])
                for j in range(4):
                    arranged[j, y] = groups[j]

    row = lax.broadcasted_iota(jnp.int32, (GROUP, 512), 0).astype(F32).astype(BF16)
    one, zero = jnp.ones((GROUP, 512), BF16), jnp.zeros((GROUP, 512), BF16)
    dense = []
    for i in range(HALF_GROUPS):
        at = pl.ds(g * HALF_GROUPS + i, 1)
        for j in range(4):
            k = jnp.concatenate([kept[j, y, at, :] for y in range(4)], axis=1)
            n = jnp.concatenate([index[j, y, at, :] for y in range(4)], axis=1).astype(jnp.int32)
            high, low = split(k)
            here = row == (n >> 6).astype(F32).astype(BF16)
            left = jnp.concatenate(
                [jnp.where(here, high, zero), jnp.where(here, low, zero)], axis=0
            )
            right = jnp.where(row == (n & 63).astype(F32).astype(BF16), one, zero)
            both = lax.dot_general(
                left, right, (((1,), (1,)), ((), ())), preferred_element_type=F32
            )
            dense.append(both[:GROUP] + both[GROUP:])
    high, low = split(jnp.concatenate(dense, axis=1))
    half = jnp.dot(
        cos_t3[...], jnp.concatenate([high, low, high], axis=0), preferred_element_type=F32
    )
    half = jnp.concatenate([half[:, i * 256 : (i + 1) * 256] for i in range(HALF_GROUPS)], axis=0)
    high, low = split(half)
    out[...] = jnp.dot(
        jnp.concatenate([high, low, high], axis=1), cos4_3[...], preferred_element_type=F32
    )


def ring_perm(flip):
    return [
        (2 * z + c, 2 * ((z + 1 - 2 * c) % CHIPS) + (1 - c if flip else c))
        for z in range(CHIPS)
        for c in range(2)
    ]


def rep_perm(dx, dy):
    return [(i, ((i // 4 + dy) % 4) * 4 + (i % 4 + dx) % 4) for i in range(N_REP)]


def on_device(inputs, cotangent, momentum, coef_index, counts):
    cosines = cosine_table()
    cos_t = jnp.asarray(cosines.T)
    parts = lambda x: (x.astype(BF16), (x - x.astype(BF16).astype(np.float32)).astype(BF16))
    high, low = parts(cosines.T)
    cos_t3 = jnp.asarray(np.concatenate([high, high, low], axis=1))
    high, low = parts(np.kron(np.eye(4, dtype=np.float32), cosines))
    cos4_3 = jnp.asarray(np.concatenate([high, high, low], axis=0))

    swap = lambda x: lax.ppermute(x, "fsdp", [(i, i ^ 1) for i in range(2 * CHIPS)])
    own_of, theirs_of = [], []

    def copied(begin, end, after, name):
        n = end - begin
        extra = COLS if begin == 0 else 0
        send, own = call(
            functools.partial(later_copy_kernel, SLOTS[begin:end]) if begin else first_copy_kernel,
            (
                jax.ShapeDtypeStruct((TOK, n * ROWS + extra), BF16),
                jax.ShapeDtypeStruct((TOK, n * ROWS), BF16),
            ),
            name,
            (1,),
            [AFTER, AFTER if begin else whole(TOK, COLS)],
            (whole(TOK, n * ROWS + extra), whole(TOK, n * ROWS)),
            scratch=[pltpu.SemaphoreType.DMA((8 * n,))],
        )(cotangent, after)
        theirs = swap(send)
        own_of.extend((own, i) for i in range(n))
        theirs_of.extend((theirs, i) for i in range(n))
        return send, theirs

    first, first_theirs = copied(0, 1, inputs, "copy0")
    second, _ = copied(1, 3, first, "copy12")

    def blocks(slot):
        specs, args = [], []
        for array, n in (own_of[slot], theirs_of[slot]):
            specs.append(pl.BlockSpec((TOK, ROWS), lambda *_, n=n: (0, n)))
            args.append(array)
        return specs, args

    message = jax.ShapeDtypeStruct((MSG, 128), jnp.int16)

    def made_tables(after):
        return call(
            tables_kernel,
            (
                jax.ShapeDtypeStruct((TILES * 256, 256), BF16),
                jax.ShapeDtypeStruct((TILES * GROUP, 256), F32),
                jax.ShapeDtypeStruct((GROUPS, 128), F32),
                jax.ShapeDtypeStruct((GROUPS, 128), F32),
            ),
            "tables",
            (1,),
            [whole(GROUPS, 4, 32), whole(GROUPS, 4), whole(GROUP, GROUP), AFTER],
            (whole(TILES * 256, 256), whole(TILES * GROUP, 256)) + (whole(GROUPS, 128),) * 2,
        )(coef_index[0], counts[0], cos_t, after)

    def momentum_t(momentum, after):
        return call(
            momentum_kernel,
            jax.ShapeDtypeStruct((COLS, ROWS), F32),
            "momentum",
            (2,),
            [pl.BlockSpec((HALF, COLS), lambda g: (g, 0)), AFTER],
            pl.BlockSpec((COLS, HALF), lambda g: (0, g)),
        )(momentum, after)

    made, sent = [], []
    for slot in range(7):
        if slot == 1:
            copied(3, 5, made[0], "copy34")
        if slot == 3:
            copied(5, 8, made[2], "copy567")
        specs, args = blocks(slot)
        if slot == 0:
            in_t, out = call(
                first_hop_kernel,
                (jax.ShapeDtypeStruct((COLS, 2 * TOK), BF16), message),
                "hop0",
                (1,),
                [whole(TOK, COLS), pl.BlockSpec((TOK, COLS), lambda g: (0, ROWS // COLS))]
                + specs
                + [AFTER],
                (whole(COLS, 2 * TOK), whole(MSG, 128)),
            )(inputs, first_theirs, *args, second)
        else:
            recv = sent[slot - 2 : slot - 1]
            after = (made[-1],)
            if slot == 3:
                basis, cw, valid, places = made_tables(made[2])
            if slot == 4:
                after = (made[-1], basis)
                mom_t = momentum_t(momentum[0], made[3])
            if slot == 5:
                after = (made[-1], mom_t)
            out = call(
                functools.partial(hop_kernel, len(after)),
                message,
                "hop%d" % slot,
                (1,),
                [AFTER] * len(after)
                + [whole(COLS, 2 * TOK)]
                + specs
                + [whole(MSG, 128)] * len(recv),
                whole(MSG, 128),
            )(*after, in_t, *args, *recv)
        made.append(out)
        sent.append(lax.ppermute(out, "fsdp", ring_perm(slot == 5)))

    specs, args = blocks(7)
    base = call(
        base_kernel,
        jax.ShapeDtypeStruct((COLS, ROWS), F32),
        "base",
        (1,),
        [whole(COLS, 2 * TOK)] + specs + [whole(MSG, 128), whole(COLS, ROWS)],
        whole(COLS, ROWS),
    )(in_t, *args, sent[5], mom_t)
    updated, kept = call(
        kept_kernel,
        (
            jax.ShapeDtypeStruct((COLS, ROWS), F32),
            jax.ShapeDtypeStruct((2 * GROUPS, 128), F32),
        ),
        "kept",
        (1,),
        [
            whole(MSG, 128),
            whole(COLS, ROWS),
            whole(TILES * 256, 256),
            whole(TILES * GROUP, 256),
            whole(GROUPS, 128),
            whole(GROUPS, 128),
        ],
        (whole(COLS, ROWS), whole(2 * GROUPS, 128)),
    )(sent[6], base, basis, cw, valid, places)
    along_x = jnp.stack(
        [kept] + [lax.ppermute(kept, "rep", rep_perm(dx, 0)) for dx in (1, 2, 3)]
    )
    kept_all = [along_x] + [lax.ppermute(along_x, "rep", rep_perm(0, dy)) for dy in (1, 2, 3)]

    new_momentum = call(
        own_kernel,
        jax.ShapeDtypeStruct((ROWS, COLS), F32),
        "own",
        (2,),
        [
            pl.BlockSpec((COLS, HALF), lambda g: (0, g)),
            whole(2 * GROUPS, 128),
            pl.BlockSpec((TILES * 128, 256), lambda g: (g, 0)),
            pl.BlockSpec((TILES * GROUP // 2, 256), lambda g: (g, 0)),
        ],
        pl.BlockSpec((HALF, COLS), lambda g: (g, 0)),
    )(updated, kept, basis, cw)

    update = call(
        update_kernel,
        jax.ShapeDtypeStruct((ROWS, COLS), F32),
        "update",
        (2,),
        [whole(4, 2 * GROUPS, 128)] * 4 + [whole(GROUP, 3 * GROUP), whole(3 * COLS, COLS)],
        pl.BlockSpec((HALF, COLS), lambda g: (g, 0)),
        scratch=[pltpu.VMEM((4, 4, GROUPS, 128), F32)] * 2,
    )(*kept_all, cos_t3, cos4_3)
    return new_momentum[None], update


def solution(mesh):
    return jax.shard_map(
        on_device,
        mesh=mesh,
        in_specs=(
            P(("fsdp", "rep"), None),
            P(("fsdp", "rep"), None),
            P("rep", "fsdp", None),
            P("rep", "fsdp", None, None),
            P("rep", "fsdp", None),
        ),
        out_specs=(P("rep", "fsdp", None), P("fsdp", None)),
        check_vma=False,
    )
```

```python
import functools
import math

import jax
import jax.numpy as jnp
import numpy as np
from jax import lax
from jax.experimental import pallas as pl
from jax.experimental.pallas import tpu as pltpu
from jax.sharding import PartitionSpec as P

GROUP = 64
DECAY = 0.9
CHIPS = 8
TOK = 128
COLS = 256
ROWS = 1792
HALF = 896
TILES = ROWS // 128
GROUPS = ROWS // GROUP
HALF_GROUPS = GROUPS // 2
GROUPS = ROWS // GROUP
HALF_GROUPS = GROUPS // 2
N_REP = 16
STEP = 64.0
TOP = 32760.0
HIGH = lax.Precision.HIGHEST
F32 = jnp.float32
BF16 = jnp.bfloat16
SLOTS = (
    (4, False),
    (3, True),
    (3, False),
    (2, True),
    (2, False),
    (1, True),
    (1, False),
    (0, False),
)
PARTS = (1, 1, 1, 1, 1, 1, 1)
VMEM_LIMIT = 24 * 1024 * 1024


def cosine_table():
    freq = np.arange(GROUP)[:, None]
    place = np.arange(GROUP)[None, :]
    table = np.cos(math.pi * (2.0 * place + 1.0) * freq / (2.0 * GROUP)) * math.sqrt(2.0 / GROUP)
    table[0] *= math.sqrt(0.5)
    return table.astype(np.float32)


def call(kernel, out_shape, name, grid, in_specs, out_specs, scalars=0, scratch=(), flops=235_000_000, nbytes=1_400_000):
    return pl.pallas_call(
        kernel,
        out_shape=out_shape,
        name=name,
        grid_spec=pltpu.PrefetchScalarGridSpec(
            num_scalar_prefetch=scalars,
            grid=grid,
            in_specs=in_specs,
            out_specs=out_specs,
            scratch_shapes=scratch,
        ),
        compiler_params=pltpu.CompilerParams(vmem_limit_bytes=VMEM_LIMIT),
        cost_estimate=pl.CostEstimate(flops=flops, bytes_accessed=nbytes, transcendentals=0),
    )


def whole(*shape):
    return pl.BlockSpec(shape, lambda *_: (0,) * len(shape))


AFTER = pl.BlockSpec(memory_space=pl.ANY)


def split(x):
    high = x.astype(BF16)
    return high, (x - high.astype(F32)).astype(BF16)


def part_rows(parts):
    return TILES // parts * COLS + 16


def read_message(parts):
    count = TILES // len(parts)
    scales = []
    for msg in parts:
        codes = msg[count * COLS :, :].astype(F32)
        scales.append(jnp.exp2(codes * (1.0 / STEP)) * (1.0 / TOP))

    def tile(j):
        n, j = j // count, j % count
        rows = parts[n][j * COLS : (j + 1) * COLS, :]
        return rows.astype(F32) * scales[n][j : j + 1, :]

    return tile


def partial_tile(in_t, own, sib, j):
    cols = slice(j * 128, (j + 1) * 128)
    tokens = jnp.concatenate([own[:, cols], sib[:, cols]], axis=0)
    return jnp.dot(in_t, tokens, preferred_element_type=F32)


def write_message(parts, tiles):
    count = TILES // len(parts)
    for n, out in enumerate(parts):
        codes = []
        for j, tile in enumerate(tiles[n * count : (n + 1) * count]):
            top = jnp.maximum(jnp.max(jnp.abs(tile), axis=0, keepdims=True), 1e-30)
            code = jnp.ceil(jnp.log2(top) * STEP)
            scaled = jnp.round(tile * (jnp.exp2(code * (-1.0 / STEP)) * TOP))
            out[j * COLS : (j + 1) * COLS, :] = scaled.astype(jnp.int32).astype(jnp.int16)
            codes.append(code)
        codes.append(jnp.zeros((16 - count, 128), F32))
        codes = jnp.concatenate(codes, axis=0)
        out[count * COLS :, :] = codes.astype(jnp.int32).astype(jnp.int16)


def copy_kernel(slots, cot, after, send, own, sems):
    place = lax.axis_index("fsdp")
    chip, core = place // 2, place % 2
    copies = []
    for whose, out in ((1 - core, send), (core, own)):
        for n, (k, flip) in enumerate(slots):
            to = (chip + k * (1 - 2 * whose) + CHIPS) % CHIPS
            start = pl.multiple_of((2 * to + (1 - whose if flip else whose)) * ROWS, 128)
            for row in range(0, TOK, 32):
                rows = slice(row, row + 32)
                copies.append(
                    (
                        cot.at[rows, pl.ds(start, ROWS)],
                        out.at[rows, n * ROWS : (n + 1) * ROWS],
                        sems.at[len(copies)],
                    )
                )
    copies = [pltpu.make_async_copy(*c) for c in copies]
    for c in copies:
        c.start()
    for c in copies:
        c.wait()


def first_hop_kernel(in_own, in_sib, own, sib, after, in_t, *outs):
    in_t[:, :TOK] = in_own[...].astype(F32).T.astype(BF16)
    in_t[:, TOK:] = in_sib[...].astype(F32).T.astype(BF16)
    both = in_t[...]
    write_message(outs, [partial_tile(both, own, sib, j) for j in range(TILES)])


def hop_kernel(n_after, n_recv, *refs):
    in_t, own, sib, *refs = refs[n_after:]
    recv, outs = refs[:n_recv], refs[n_recv:]
    both = in_t[...]
    tiles = [partial_tile(both, own, sib, j) for j in range(TILES)]
    if recv:
        read = read_message(recv)
        tiles = [tile + read(j) for j, tile in enumerate(tiles)]
    write_message(outs, tiles)


def tables_kernel(listed, counts, cos_t, after, basis, cw, valid, places):
    row = lax.broadcasted_iota(jnp.int32, (GROUP, 512), 0)
    lane = lax.broadcasted_iota(jnp.int32, (GROUP, 256), 1)
    index = jnp.concatenate([listed[:, j, :] for j in range(4)], axis=1)
    places[...] = index.astype(F32)
    for p in range(TILES):
        n = jnp.concatenate([index[2 * p : 2 * p + 1, :], index[2 * p + 1 : 2 * p + 2, :]], axis=1)
        onehot = jnp.where(row == jnp.concatenate([n >> 6, n & 63], axis=1), 1.0, 0.0).astype(F32)
        both = jnp.dot(cos_t[...], onehot, precision=HIGH, preferred_element_type=F32)
        cw[p * GROUP : (p + 1) * GROUP, :] = both[:, 256:]
        cu = both[:, :256]
        diagonal = jnp.concatenate(
            [jnp.where(lane < 128, cu, 0.0), jnp.where(lane >= 128, cu, 0.0)], axis=0
        )
        high, low = split(diagonal)
        basis[p * 256 : p * 256 + 128, :] = high
        basis[p * 256 + 128 : (p + 1) * 256, :] = low
    slot = lax.broadcasted_iota(jnp.int32, (GROUPS, 128), 1)
    limit = jnp.zeros((GROUPS, 128), jnp.int32)
    for j in range(4):
        limit = jnp.where((slot >> 5) == j, counts[:, j : j + 1], limit)
    valid[...] = jnp.where((slot & 31) < limit, 1.0, 0.0).astype(F32)


def momentum_kernel(momentum, after, out):
    out[...] = (DECAY * momentum[...]).T


def by_column_group(rows):
    block = lax.broadcasted_iota(jnp.int32, rows[0].shape, 1) >> 5
    out = []
    for j in range(4):
        total = rows[j]
        for b in range(4):
            if b != j:
                total = jnp.where(block == b, pltpu.roll(rows[b], (32 * (b - j)) % 128, 1), total)
        out.append(total)
    return out


def base_kernel(after1, after2, after3, in_t, own, sib, mom_t, *refs):
    both = in_t[...]
    out = refs[-1]
    read = read_message(refs[:-1])
    for j in range(TILES):
        cols = slice(j * 128, (j + 1) * 128)
        out[:, cols] = partial_tile(both, own, sib, j) + mom_t[:, cols] + read(j)


def kept_kernel(base, basis, cw, valid, *refs):
    updated, kept = refs[-2:]
    read = read_message(refs[:-2])
    column = (lax.broadcasted_iota(jnp.int32, (GROUP, 256), 1) & 127) >> 5
    for p in range(TILES):
        cols = slice(p * 128, (p + 1) * 128)
        tile = base[:, cols] + read(p)
        updated[:, cols] = tile
        high, low = split(tile)
        b_high = basis[p * 256 : p * 256 + 128, :]
        b_low = basis[p * 256 + 128 : (p + 1) * 256, :]
        seen = jnp.dot(
            jnp.concatenate([high, low, high], axis=1),
            jnp.concatenate([b_high, b_high, b_low], axis=0),
            preferred_element_type=F32,
        )
        mine = seen[:GROUP]
        for c in range(1, 4):
            mine = jnp.where(column == c, seen[c * GROUP : (c + 1) * GROUP], mine)
        picked = jnp.sum(mine * cw[p * GROUP : (p + 1) * GROUP, :], axis=0, keepdims=True)
        for i in range(2):
            at = slice(2 * p + i, 2 * p + i + 1)
            half = picked[:, i * 128 : (i + 1) * 128]
            kept[at, :] = jnp.where(valid[at, :] > 0.0, half, 0.0)


def own_kernel(updated, kept, basis, cw, out, done):
    done[...] = jnp.zeros(done.shape, F32)
    g = pl.program_id(0)
    column = (lax.broadcasted_iota(jnp.int32, (GROUP, 256), 1) & 127) >> 5
    for p in range(TILES // 2):
        k = jnp.concatenate(
            [kept[pl.ds(2 * (g * (TILES // 2) + p) + i, 1), :] for i in range(2)], axis=1
        )
        weighted = cw[p * GROUP : (p + 1) * GROUP, :] * k
        spread = jnp.concatenate([jnp.where(column == c, weighted, 0.0) for c in range(4)], axis=0)
        high, low = split(spread)
        b_high = basis[p * 256 : p * 256 + 128, :]
        b_low = basis[p * 256 + 128 : (p + 1) * 256, :]
        decoded = lax.dot_general(
            jnp.concatenate([high, low, high], axis=1),
            jnp.concatenate([b_high, b_high, b_low], axis=1),
            (((1,), (1,)), ((), ())),
            preferred_element_type=F32,
        )
        cols = slice(p * 128, (p + 1) * 128)
        out[cols, :] = (updated[:, cols] - decoded).T


def arrange_kernel(k0, k1, k2, k3, after, out):
    for j, rows in enumerate(by_column_group([k0[...], k1[...], k2[...], k3[...]])):
        out[j] = rows


def update_kernel(k0, k1, k2, k3, n0, n1, n2, n3, cos_t3, cos4_3, out):
    g = pl.program_id(0)
    row = lax.broadcasted_iota(jnp.int32, (GROUP, 512), 0).astype(F32).astype(BF16)
    one, zero = jnp.ones((GROUP, 512), BF16), jnp.zeros((GROUP, 512), BF16)
    dense = []
    for i in range(HALF_GROUPS):
        at = pl.ds(g * HALF_GROUPS + i, 1)
        for j in range(4):
            k = jnp.concatenate([ref[j, at, :] for ref in (k0, k1, k2, k3)], axis=1)
            n = jnp.concatenate([ref[j, at, :] for ref in (n0, n1, n2, n3)], axis=1)
            n = n.astype(jnp.int32)
            high, low = split(k)
            here = row == (n >> 6).astype(F32).astype(BF16)
            left = jnp.concatenate(
                [jnp.where(here, high, zero), jnp.where(here, low, zero)], axis=0
            )
            right = jnp.where(row == (n & 63).astype(F32).astype(BF16), one, zero)
            both = lax.dot_general(
                left, right, (((1,), (1,)), ((), ())), preferred_element_type=F32
            )
            dense.append(both[:GROUP] + both[GROUP:])
    high, low = split(jnp.concatenate(dense, axis=1))
    half = jnp.dot(
        cos_t3[...], jnp.concatenate([high, low, high], axis=0), preferred_element_type=F32
    )
    half = jnp.concatenate([half[:, i * 256 : (i + 1) * 256] for i in range(HALF_GROUPS)], axis=0)
    high, low = split(half)
    out[...] = jnp.dot(
        jnp.concatenate([high, low, high], axis=1), cos4_3[...], preferred_element_type=F32
    )


def ring_perm(flip):
    return [
        (2 * z + c, 2 * ((z + 1 - 2 * c) % CHIPS) + (1 - c if flip else c))
        for z in range(CHIPS)
        for c in range(2)
    ]


def rep_perm(dx, dy):
    return [(i, ((i // 4 + dy) % 4) * 4 + (i % 4 + dx) % 4) for i in range(N_REP)]


def on_device(inputs, cotangent, momentum, coef_index, counts):
    cosines = cosine_table()
    cos_t = jnp.asarray(cosines.T)
    parts = lambda x: (x.astype(BF16), (x - x.astype(BF16).astype(np.float32)).astype(BF16))
    high, low = parts(cosines.T)
    cos_t3 = jnp.asarray(np.concatenate([high, high, low], axis=1))
    high, low = parts(np.kron(np.eye(4, dtype=np.float32), cosines))
    cos4_3 = jnp.asarray(np.concatenate([high, high, low], axis=0))

    swap = lambda x: lax.ppermute(x, "fsdp", [(i, i ^ 1) for i in range(2 * CHIPS)])
    own_of, theirs_of = [], []

    def exchanged(send, own, n):
        theirs = swap(send)
        own_of.extend((own, i) for i in range(n))
        theirs_of.extend((theirs, i) for i in range(n))
        return theirs

    def copied(begin, end, after, name):
        n = end - begin
        shape = jax.ShapeDtypeStruct((TOK, n * ROWS), BF16)
        send, own = call(
            functools.partial(copy_kernel, SLOTS[begin:end]),
            (shape, shape),
            name,
            (1,),
            [AFTER, AFTER],
            (whole(TOK, n * ROWS), whole(TOK, n * ROWS)),
            scratch=[pltpu.SemaphoreType.DMA((8 * n,))],
        )(cotangent, after)
        exchanged(send, own, n)
        return send

    place = lax.axis_index("fsdp")
    across = (place + CHIPS) % (2 * CHIPS)
    first, first_own = (
        lax.dynamic_slice(cotangent, (0, block * ROWS), (TOK, ROWS))
        for block in (across ^ 1, across)
    )
    exchanged(first, first_own, 1)
    in_sib = swap(inputs)
    second = copied(1, 3, first, "copy12")

    def blocks(slot):
        specs, args = [], []
        for array, n in (own_of[slot], theirs_of[slot]):
            specs.append(pl.BlockSpec((TOK, ROWS), lambda *_, n=n: (0, n)))
            args.append(array)
        return specs, args

    def message(slot):
        rows = part_rows(PARTS[slot])
        return (
            (jax.ShapeDtypeStruct((rows, 128), jnp.int16),) * PARTS[slot],
            (whole(rows, 128),) * PARTS[slot],
        )

    def made_tables(after):
        return call(
            tables_kernel,
            (
                jax.ShapeDtypeStruct((TILES * 256, 256), BF16),
                jax.ShapeDtypeStruct((TILES * GROUP, 256), F32),
                jax.ShapeDtypeStruct((GROUPS, 128), F32),
                jax.ShapeDtypeStruct((GROUPS, 128), F32),
            ),
            "tables",
            (1,),
            [whole(GROUPS, 4, 32), whole(GROUPS, 4), whole(GROUP, GROUP), AFTER],
            (whole(TILES * 256, 256), whole(TILES * GROUP, 256)) + (whole(GROUPS, 128),) * 2,
        )(coef_index[0], counts[0], cos_t, after)

    def momentum_t(momentum, after):
        return call(
            momentum_kernel,
            jax.ShapeDtypeStruct((COLS, ROWS), F32),
            "momentum",
            (2,),
            [pl.BlockSpec((HALF, COLS), lambda g: (g, 0)), AFTER],
            pl.BlockSpec((COLS, HALF), lambda g: (0, g)),
        )(momentum, after)

    def along_x(rows):
        return [lax.ppermute(rows, "rep", rep_perm(dx, 0)) for dx in (1, 2, 3)]

    def along_y(rows):
        return [rows] + [lax.ppermute(rows, "rep", rep_perm(0, dy)) for dy in (1, 2, 3)]

    def arranged(rows, from_x, after, name):
        return call(
            arrange_kernel,
            jax.ShapeDtypeStruct((4, GROUPS, 128), F32),
            name,
            (1,),
            [whole(GROUPS, 128)] * 4 + [AFTER],
            whole(4, GROUPS, 128),
        )(rows, *from_x, after)

    made, sent = [], []
    for slot in range(7):
        if slot == 1:
            copied(3, 5, made[0], "copy34")
        if slot == 3:
            copied(5, 8, made[2], "copy567")
        specs, args = blocks(slot)
        shapes, out_specs = message(slot)
        if slot == 0:
            in_t, *outs = call(
                first_hop_kernel,
                (jax.ShapeDtypeStruct((COLS, 2 * TOK), BF16),) + shapes,
                "hop0",
                (1,),
                [whole(TOK, COLS), whole(TOK, COLS)]
                + specs
                + [AFTER],
                (whole(COLS, 2 * TOK),) + out_specs,
            )(inputs, in_sib, *args, second)
        else:
            recv, recv_specs = ((), ()) if slot < 2 else (sent[slot - 2], message(slot - 2)[1])
            after = (made[-1],)
            if slot == 2:
                basis, cw, valid, places = made_tables(made[1])
                places_x = along_x(places)
            if slot == 3:
                after = (made[-1], basis)
                mom_t = momentum_t(momentum[0], made[2])
            if slot == 4:
                after = (made[-1], mom_t)
                places_all = along_y(arranged(places, places_x, made[3], "places"))
            if slot == 5:
                after = (made[-1], places_all[0])
            outs = call(
                functools.partial(hop_kernel, len(after), len(recv)),
                shapes,
                "hop%d" % slot,
                (1,),
                [AFTER] * len(after)
                + [whole(COLS, 2 * TOK)]
                + specs
                + list(recv_specs),
                out_specs,
            )(*after, in_t, *args, *recv)
        made.append(outs[-1])
        sent.append([lax.ppermute(out, "fsdp", ring_perm(slot == 5)) for out in outs])

    specs, args = blocks(7)
    base = call(
        base_kernel,
        jax.ShapeDtypeStruct((COLS, ROWS), F32),
        "base",
        (1,),
        [AFTER] * 3 + [whole(COLS, 2 * TOK)] + specs + [whole(COLS, ROWS)] + list(message(5)[1]),
        whole(COLS, ROWS),
    )(*places_all[1:], in_t, *args, mom_t, *sent[5])
    updated, kept = call(
        kept_kernel,
        (
            jax.ShapeDtypeStruct((COLS, ROWS), F32),
            jax.ShapeDtypeStruct((GROUPS, 128), F32),
        ),
        "kept",
        (1,),
        [
            whole(COLS, ROWS),
            whole(TILES * 256, 256),
            whole(TILES * GROUP, 256),
            whole(GROUPS, 128),
        ]
        + list(message(6)[1]),
        (whole(COLS, ROWS), whole(GROUPS, 128)),
    )(base, basis, cw, valid, *sent[6])
    from_x = along_x(kept)
    new_momentum, own_done = call(
        own_kernel,
        (jax.ShapeDtypeStruct((ROWS, COLS), F32), jax.ShapeDtypeStruct((8, 128), F32)),
        "own",
        (2,),
        [
            pl.BlockSpec((COLS, HALF), lambda g: (0, g)),
            whole(GROUPS, 128),
            pl.BlockSpec((TILES * 128, 256), lambda g: (g, 0)),
            pl.BlockSpec((TILES * GROUP // 2, 256), lambda g: (g, 0)),
        ],
        (pl.BlockSpec((HALF, COLS), lambda g: (g, 0)), whole(8, 128)),
    )(updated, kept, basis, cw)

    kept_all = along_y(arranged(kept, from_x, own_done, "arrange"))

    update = call(
        update_kernel,
        jax.ShapeDtypeStruct((ROWS, COLS), F32),
        "update",
        (2,),
        [whole(4, GROUPS, 128)] * 8 + [whole(GROUP, 3 * GROUP), whole(3 * COLS, COLS)],
        pl.BlockSpec((HALF, COLS), lambda g: (g, 0)),
    )(*kept_all, *places_all, cos_t3, cos4_3)
    return new_momentum[None], update


def solution(mesh):
    return jax.shard_map(
        on_device,
        mesh=mesh,
        in_specs=(
            P(("fsdp", "rep"), None),
            P(("fsdp", "rep"), None),
            P("rep", "fsdp", None),
            P("rep", "fsdp", None, None),
            P("rep", "fsdp", None),
        ),
        out_specs=(P("rep", "fsdp", None), P("fsdp", None)),
        check_vma=False,
    )
```

```python
import functools
import math

import jax
import jax.numpy as jnp
import numpy as np
from jax import lax
from jax.experimental import pallas as pl
from jax.experimental.pallas import tpu as pltpu
from jax.sharding import PartitionSpec as P

GROUP = 64
DECAY = 0.9
CHIPS = 8
TOK = 128
COLS = 256
ROWS = 1792
HALF = 896
TILES = ROWS // 128
GROUPS = ROWS // GROUP
HALF_GROUPS = GROUPS // 2
GROUPS = ROWS // GROUP
HALF_GROUPS = GROUPS // 2
N_REP = 16
STEP = 64.0
TOP = 32760.0
HIGH = lax.Precision.HIGHEST
F32 = jnp.float32
BF16 = jnp.bfloat16
SLOTS = (
    (4, False),
    (3, True),
    (3, False),
    (2, True),
    (2, False),
    (1, True),
    (1, False),
    (0, False),
)
PARTS = (1, 1, 1, 1, 1, 1, 1)
VMEM_LIMIT = 24 * 1024 * 1024


def cosine_table():
    freq = np.arange(GROUP)[:, None]
    place = np.arange(GROUP)[None, :]
    table = np.cos(math.pi * (2.0 * place + 1.0) * freq / (2.0 * GROUP)) * math.sqrt(2.0 / GROUP)
    table[0] *= math.sqrt(0.5)
    return table.astype(np.float32)


def call(kernel, out_shape, name, grid, in_specs, out_specs, scalars=0, scratch=(), flops=235_000_000, nbytes=1_400_000):
    return pl.pallas_call(
        kernel,
        out_shape=out_shape,
        name=name,
        grid_spec=pltpu.PrefetchScalarGridSpec(
            num_scalar_prefetch=scalars,
            grid=grid,
            in_specs=in_specs,
            out_specs=out_specs,
            scratch_shapes=scratch,
        ),
        compiler_params=pltpu.CompilerParams(vmem_limit_bytes=VMEM_LIMIT),
        cost_estimate=pl.CostEstimate(flops=flops, bytes_accessed=nbytes, transcendentals=0),
    )


def whole(*shape):
    return pl.BlockSpec(shape, lambda *_: (0,) * len(shape))


AFTER = pl.BlockSpec(memory_space=pl.ANY)


def split(x):
    high = x.astype(BF16)
    return high, (x - high.astype(F32)).astype(BF16)


def part_rows(parts):
    return TILES // parts * COLS + 16


def read_message(parts):
    count = TILES // len(parts)
    scales = []
    for msg in parts:
        codes = msg[count * COLS :, :].astype(F32)
        scales.append(jnp.exp2(codes * (1.0 / STEP)) * (1.0 / TOP))

    def tile(j):
        n, j = j // count, j % count
        rows = parts[n][j * COLS : (j + 1) * COLS, :]
        return rows.astype(F32) * scales[n][j : j + 1, :]

    return tile


def partial_tile(in_t, own, sib, j):
    cols = slice(j * 128, (j + 1) * 128)
    tokens = jnp.concatenate([own[:, cols], sib[:, cols]], axis=0)
    return jnp.dot(in_t, tokens, preferred_element_type=F32)


def write_message(parts, tiles):
    count = TILES // len(parts)
    for n, out in enumerate(parts):
        codes = []
        for j, tile in enumerate(tiles[n * count : (n + 1) * count]):
            top = jnp.maximum(jnp.max(jnp.abs(tile), axis=0, keepdims=True), 1e-30)
            code = jnp.ceil(jnp.log2(top) * STEP)
            scaled = jnp.round(tile * (jnp.exp2(code * (-1.0 / STEP)) * TOP))
            out[j * COLS : (j + 1) * COLS, :] = scaled.astype(jnp.int32).astype(jnp.int16)
            codes.append(code)
        codes.append(jnp.zeros((16 - count, 128), F32))
        codes = jnp.concatenate(codes, axis=0)
        out[count * COLS :, :] = codes.astype(jnp.int32).astype(jnp.int16)


def copy_kernel(slots, cot, after, send, own, sems):
    place = lax.axis_index("fsdp")
    chip, core = place // 2, place % 2
    copies = []
    for whose, out in ((1 - core, send), (core, own)):
        for n, (k, flip) in enumerate(slots):
            to = (chip + k * (1 - 2 * whose) + CHIPS) % CHIPS
            start = pl.multiple_of((2 * to + (1 - whose if flip else whose)) * ROWS, 128)
            for row in range(0, TOK, 32):
                rows = slice(row, row + 32)
                copies.append(
                    (
                        cot.at[rows, pl.ds(start, ROWS)],
                        out.at[rows, n * ROWS : (n + 1) * ROWS],
                        sems.at[len(copies)],
                    )
                )
    copies = [pltpu.make_async_copy(*c) for c in copies]
    for c in copies:
        c.start()
    for c in copies:
        c.wait()


def first_hop_kernel(in_own, in_sib, own, sib, in_t, *outs):
    in_t[:, :TOK] = in_own[...].astype(F32).T.astype(BF16)
    in_t[:, TOK:] = in_sib[...].astype(F32).T.astype(BF16)
    both = in_t[...]
    write_message(outs, [partial_tile(both, own, sib, j) for j in range(TILES)])


def hop_kernel(n_after, n_recv, *refs):
    in_t, own, sib, *refs = refs[n_after:]
    recv, outs = refs[:n_recv], refs[n_recv:]
    both = in_t[...]
    tiles = [partial_tile(both, own, sib, j) for j in range(TILES)]
    if recv:
        read = read_message(recv)
        tiles = [tile + read(j) for j, tile in enumerate(tiles)]
    write_message(outs, tiles)


def tables_kernel(listed, counts, cos_t, after, basis, cw, valid, places):
    row = lax.broadcasted_iota(jnp.int32, (GROUP, 512), 0)
    lane = lax.broadcasted_iota(jnp.int32, (GROUP, 256), 1)
    index = jnp.concatenate([listed[:, j, :] for j in range(4)], axis=1)
    places[...] = index.astype(F32)
    for p in range(TILES):
        n = jnp.concatenate([index[2 * p : 2 * p + 1, :], index[2 * p + 1 : 2 * p + 2, :]], axis=1)
        onehot = jnp.where(row == jnp.concatenate([n >> 6, n & 63], axis=1), 1.0, 0.0).astype(F32)
        both = jnp.dot(cos_t[...], onehot, precision=HIGH, preferred_element_type=F32)
        cw[p * GROUP : (p + 1) * GROUP, :] = both[:, 256:]
        cu = both[:, :256]
        diagonal = jnp.concatenate(
            [jnp.where(lane < 128, cu, 0.0), jnp.where(lane >= 128, cu, 0.0)], axis=0
        )
        high, low = split(diagonal)
        basis[p * 256 : p * 256 + 128, :] = high
        basis[p * 256 + 128 : (p + 1) * 256, :] = low
    slot = lax.broadcasted_iota(jnp.int32, (GROUPS, 128), 1)
    limit = jnp.zeros((GROUPS, 128), jnp.int32)
    for j in range(4):
        limit = jnp.where((slot >> 5) == j, counts[:, j : j + 1], limit)
    valid[...] = jnp.where((slot & 31) < limit, 1.0, 0.0).astype(F32)


def momentum_kernel(momentum, after, out):
    out[...] = (DECAY * momentum[...]).T


def by_column_group(rows):
    block = lax.broadcasted_iota(jnp.int32, rows[0].shape, 1) >> 5
    out = []
    for j in range(4):
        total = rows[j]
        for b in range(4):
            if b != j:
                total = jnp.where(block == b, pltpu.roll(rows[b], (32 * (b - j)) % 128, 1), total)
        out.append(total)
    return out


def base_kernel(after1, after2, after3, in_t, own, sib, mom_t, *refs):
    both = in_t[...]
    out = refs[-1]
    read = read_message(refs[:-1])
    for j in range(TILES):
        cols = slice(j * 128, (j + 1) * 128)
        out[:, cols] = partial_tile(both, own, sib, j) + mom_t[:, cols] + read(j)


def kept_kernel(base, basis, cw, valid, *refs):
    updated, kept = refs[-2:]
    read = read_message(refs[:-2])
    column = (lax.broadcasted_iota(jnp.int32, (GROUP, 256), 1) & 127) >> 5
    for p in range(TILES):
        cols = slice(p * 128, (p + 1) * 128)
        tile = base[:, cols] + read(p)
        updated[:, cols] = tile
        high, low = split(tile)
        b_high = basis[p * 256 : p * 256 + 128, :]
        b_low = basis[p * 256 + 128 : (p + 1) * 256, :]
        seen = jnp.dot(
            jnp.concatenate([high, low, high], axis=1),
            jnp.concatenate([b_high, b_high, b_low], axis=0),
            preferred_element_type=F32,
        )
        mine = seen[:GROUP]
        for c in range(1, 4):
            mine = jnp.where(column == c, seen[c * GROUP : (c + 1) * GROUP], mine)
        picked = jnp.sum(mine * cw[p * GROUP : (p + 1) * GROUP, :], axis=0, keepdims=True)
        for i in range(2):
            at = slice(2 * p + i, 2 * p + i + 1)
            half = picked[:, i * 128 : (i + 1) * 128]
            kept[at, :] = jnp.where(valid[at, :] > 0.0, half, 0.0)


def own_kernel(updated, kept, basis, cw, out, done):
    done[...] = jnp.zeros(done.shape, F32)
    g = pl.program_id(0)
    column = (lax.broadcasted_iota(jnp.int32, (GROUP, 256), 1) & 127) >> 5
    for p in range(TILES // 2):
        k = jnp.concatenate(
            [kept[pl.ds(2 * (g * (TILES // 2) + p) + i, 1), :] for i in range(2)], axis=1
        )
        weighted = cw[p * GROUP : (p + 1) * GROUP, :] * k
        spread = jnp.concatenate([jnp.where(column == c, weighted, 0.0) for c in range(4)], axis=0)
        high, low = split(spread)
        b_high = basis[p * 256 : p * 256 + 128, :]
        b_low = basis[p * 256 + 128 : (p + 1) * 256, :]
        decoded = lax.dot_general(
            jnp.concatenate([high, low, high], axis=1),
            jnp.concatenate([b_high, b_high, b_low], axis=1),
            (((1,), (1,)), ((), ())),
            preferred_element_type=F32,
        )
        cols = slice(p * 128, (p + 1) * 128)
        out[cols, :] = (updated[:, cols] - decoded).T


def arrange_kernel(k0, k1, k2, k3, after, out):
    for j, rows in enumerate(by_column_group([k0[...], k1[...], k2[...], k3[...]])):
        out[j] = rows


def update_kernel(k0, k1, k2, k3, n0, n1, n2, n3, cos_t3, cos4_3, out):
    g = pl.program_id(0)
    row = lax.broadcasted_iota(jnp.int32, (GROUP, 512), 0).astype(F32).astype(BF16)
    one, zero = jnp.ones((GROUP, 512), BF16), jnp.zeros((GROUP, 512), BF16)
    dense = []
    for i in range(HALF_GROUPS):
        at = pl.ds(g * HALF_GROUPS + i, 1)
        for j in range(4):
            k = jnp.concatenate([ref[j, at, :] for ref in (k0, k1, k2, k3)], axis=1)
            n = jnp.concatenate([ref[j, at, :] for ref in (n0, n1, n2, n3)], axis=1)
            n = n.astype(jnp.int32)
            high, low = split(k)
            here = row == (n >> 6).astype(F32).astype(BF16)
            left = jnp.concatenate(
                [jnp.where(here, high, zero), jnp.where(here, low, zero)], axis=0
            )
            right = jnp.where(row == (n & 63).astype(F32).astype(BF16), one, zero)
            both = lax.dot_general(
                left, right, (((1,), (1,)), ((), ())), preferred_element_type=F32
            )
            dense.append(both[:GROUP] + both[GROUP:])
    high, low = split(jnp.concatenate(dense, axis=1))
    half = jnp.dot(
        cos_t3[...], jnp.concatenate([high, low, high], axis=0), preferred_element_type=F32
    )
    half = jnp.concatenate([half[:, i * 256 : (i + 1) * 256] for i in range(HALF_GROUPS)], axis=0)
    high, low = split(half)
    out[...] = jnp.dot(
        jnp.concatenate([high, low, high], axis=1), cos4_3[...], preferred_element_type=F32
    )


def ring_perm(flip):
    return [
        (2 * z + c, 2 * ((z + 1 - 2 * c) % CHIPS) + (1 - c if flip else c))
        for z in range(CHIPS)
        for c in range(2)
    ]


def rep_perm(dx, dy):
    return [(i, ((i // 4 + dy) % 4) * 4 + (i % 4 + dx) % 4) for i in range(N_REP)]


def on_device(inputs, cotangent, momentum, coef_index, counts):
    cosines = cosine_table()
    cos_t = jnp.asarray(cosines.T)
    parts = lambda x: (x.astype(BF16), (x - x.astype(BF16).astype(np.float32)).astype(BF16))
    high, low = parts(cosines.T)
    cos_t3 = jnp.asarray(np.concatenate([high, high, low], axis=1))
    high, low = parts(np.kron(np.eye(4, dtype=np.float32), cosines))
    cos4_3 = jnp.asarray(np.concatenate([high, high, low], axis=0))

    swap = lambda x: lax.ppermute(x, "fsdp", [(i, i ^ 1) for i in range(2 * CHIPS)])
    own_of, theirs_of = [], []

    def exchanged(send, own, n):
        theirs = swap(send)
        own_of.extend((own, i) for i in range(n))
        theirs_of.extend((theirs, i) for i in range(n))
        return theirs

    def copied(begin, end, after, name):
        n = end - begin
        shape = jax.ShapeDtypeStruct((TOK, n * ROWS), BF16)
        send, own = call(
            functools.partial(copy_kernel, SLOTS[begin:end]),
            (shape, shape),
            name,
            (1,),
            [AFTER, AFTER],
            (whole(TOK, n * ROWS), whole(TOK, n * ROWS)),
            scratch=[pltpu.SemaphoreType.DMA((8 * n,))],
        )(cotangent, after)
        exchanged(send, own, n)
        return send

    place = lax.axis_index("fsdp")

    def sliced(slot, whose):
        k, flip = SLOTS[slot]
        to = (place // 2 + k * (1 - 2 * whose) + CHIPS) % CHIPS
        start = (2 * to + (1 - whose if flip else whose)) * ROWS
        return lax.dynamic_slice(cotangent, (0, start), (TOK, ROWS))

    exchanged(sliced(0, 1 - place % 2), sliced(0, place % 2), 1)
    in_sib = swap(inputs)
    for slot in (1, 2):
        exchanged(sliced(slot, 1 - place % 2), sliced(slot, place % 2), 1)

    def blocks(slot):
        specs, args = [], []
        for array, n in (own_of[slot], theirs_of[slot]):
            specs.append(pl.BlockSpec((TOK, ROWS), lambda *_, n=n: (0, n)))
            args.append(array)
        return specs, args

    def message(slot):
        rows = part_rows(PARTS[slot])
        return (
            (jax.ShapeDtypeStruct((rows, 128), jnp.int16),) * PARTS[slot],
            (whole(rows, 128),) * PARTS[slot],
        )

    def made_tables(after):
        return call(
            tables_kernel,
            (
                jax.ShapeDtypeStruct((TILES * 256, 256), BF16),
                jax.ShapeDtypeStruct((TILES * GROUP, 256), F32),
                jax.ShapeDtypeStruct((GROUPS, 128), F32),
                jax.ShapeDtypeStruct((GROUPS, 128), F32),
            ),
            "tables",
            (1,),
            [whole(GROUPS, 4, 32), whole(GROUPS, 4), whole(GROUP, GROUP), AFTER],
            (whole(TILES * 256, 256), whole(TILES * GROUP, 256)) + (whole(GROUPS, 128),) * 2,
        )(coef_index[0], counts[0], cos_t, after)

    def momentum_t(momentum, after):
        return call(
            momentum_kernel,
            jax.ShapeDtypeStruct((COLS, ROWS), F32),
            "momentum",
            (2,),
            [pl.BlockSpec((HALF, COLS), lambda g: (g, 0)), AFTER],
            pl.BlockSpec((COLS, HALF), lambda g: (0, g)),
        )(momentum, after)

    def along_x(rows):
        return [lax.ppermute(rows, "rep", rep_perm(dx, 0)) for dx in (1, 2, 3)]

    def along_y(rows):
        return [rows] + [lax.ppermute(rows, "rep", rep_perm(0, dy)) for dy in (1, 2, 3)]

    def arranged(rows, from_x, after, name):
        return call(
            arrange_kernel,
            jax.ShapeDtypeStruct((4, GROUPS, 128), F32),
            name,
            (1,),
            [whole(GROUPS, 128)] * 4 + [AFTER],
            whole(4, GROUPS, 128),
        )(rows, *from_x, after)

    made, sent = [], []
    for slot in range(7):
        if slot == 1:
            copied(3, 5, made[0], "copy34")
        if slot == 3:
            copied(5, 8, made[2], "copy567")
        specs, args = blocks(slot)
        shapes, out_specs = message(slot)
        if slot == 0:
            in_t, *outs = call(
                first_hop_kernel,
                (jax.ShapeDtypeStruct((COLS, 2 * TOK), BF16),) + shapes,
                "hop0",
                (1,),
                [whole(TOK, COLS), whole(TOK, COLS)]
                + specs,
                (whole(COLS, 2 * TOK),) + out_specs,
            )(inputs, in_sib, *args)
        else:
            recv, recv_specs = ((), ()) if slot < 2 else (sent[slot - 2], message(slot - 2)[1])
            after = (made[-1],)
            if slot == 2:
                basis, cw, valid, places = made_tables(made[1])
                places_x = along_x(places)
            if slot == 3:
                after = (made[-1], basis)
                mom_t = momentum_t(momentum[0], made[2])
            if slot == 4:
                after = (made[-1], mom_t)
                places_all = along_y(arranged(places, places_x, made[3], "places"))
            if slot == 5:
                after = (made[-1], places_all[0])
            outs = call(
                functools.partial(hop_kernel, len(after), len(recv)),
                shapes,
                "hop%d" % slot,
                (1,),
                [AFTER] * len(after)
                + [whole(COLS, 2 * TOK)]
                + specs
                + list(recv_specs),
                out_specs,
            )(*after, in_t, *args, *recv)
        made.append(outs[-1])
        sent.append([lax.ppermute(out, "fsdp", ring_perm(slot == 5)) for out in outs])

    specs, args = blocks(7)
    base = call(
        base_kernel,
        jax.ShapeDtypeStruct((COLS, ROWS), F32),
        "base",
        (1,),
        [AFTER] * 3 + [whole(COLS, 2 * TOK)] + specs + [whole(COLS, ROWS)] + list(message(5)[1]),
        whole(COLS, ROWS),
    )(*places_all[1:], in_t, *args, mom_t, *sent[5])
    updated, kept = call(
        kept_kernel,
        (
            jax.ShapeDtypeStruct((COLS, ROWS), F32),
            jax.ShapeDtypeStruct((GROUPS, 128), F32),
        ),
        "kept",
        (1,),
        [
            whole(COLS, ROWS),
            whole(TILES * 256, 256),
            whole(TILES * GROUP, 256),
            whole(GROUPS, 128),
        ]
        + list(message(6)[1]),
        (whole(COLS, ROWS), whole(GROUPS, 128)),
    )(base, basis, cw, valid, *sent[6])
    from_x = along_x(kept)
    new_momentum, own_done = call(
        own_kernel,
        (jax.ShapeDtypeStruct((ROWS, COLS), F32), jax.ShapeDtypeStruct((8, 128), F32)),
        "own",
        (2,),
        [
            pl.BlockSpec((COLS, HALF), lambda g: (0, g)),
            whole(GROUPS, 128),
            pl.BlockSpec((TILES * 128, 256), lambda g: (g, 0)),
            pl.BlockSpec((TILES * GROUP // 2, 256), lambda g: (g, 0)),
        ],
        (pl.BlockSpec((HALF, COLS), lambda g: (g, 0)), whole(8, 128)),
    )(updated, kept, basis, cw)

    kept_all = along_y(arranged(kept, from_x, own_done, "arrange"))

    update = call(
        update_kernel,
        jax.ShapeDtypeStruct((ROWS, COLS), F32),
        "update",
        (2,),
        [whole(4, GROUPS, 128)] * 8 + [whole(GROUP, 3 * GROUP), whole(3 * COLS, COLS)],
        pl.BlockSpec((HALF, COLS), lambda g: (g, 0)),
    )(*kept_all, *places_all, cos_t3, cos4_3)
    return new_momentum[None], update


def solution(mesh):
    return jax.shard_map(
        on_device,
        mesh=mesh,
        in_specs=(
            P(("fsdp", "rep"), None),
            P(("fsdp", "rep"), None),
            P("rep", "fsdp", None),
            P("rep", "fsdp", None, None),
            P("rep", "fsdp", None),
        ),
        out_specs=(P("rep", "fsdp", None), P("fsdp", None)),
        check_vma=False,
    )
```
